256 devices in a mesh: row: 32 (over z, y), col: 8 (over x, core).
Axes of the slice: x: 4, y: 4, z: 8, core: 2. Of those that a mesh axis runs over, the one named last changes fastest.
Arguments:
- blocks: bfloat16 [32, 8, 224, 128, 128], P('row', 'col'), may hold values from -0.125 to 0.125
- block_rows: int32 [32, 8, 224], P('row', 'col'), may hold values from 0 to 15, as said below
- block_cols: int32 [32, 8, 224], P('row', 'col'), may hold values from 0 to 63, as said below
- live_counts: int32 [32, 8], P('row', 'col'), may hold values from 64 to 224, as said below
- omega: bfloat16 [65536, 256], P(('col', 'row')), may hold values from -6 to 6
- row_scale: float32 [65536], P(('row', 'col')), may hold values from 0.1 to 12
Outputs:
- basis: float32 [65536, 256], P(('row', 'col'))
- factor: float32 [256, 256], replicated
The draws below stay inside these ranges and needn't reach their ends.
Inputs may be any that keep to these rules, and one draw needn't show every extreme that they name: `block_rows`: local row block of each slot; in each device's first 16 slots every local row block stands once. `block_cols`: local column block of each slot; in each device's first 64 slots every local column block stands once. `live_counts`: at least max(16, 64) on every device; some device has all 224 slots live.
All inputs are finite; a program needn't handle non-finite values.
Results may differ from the reference program's by a relative error of at most 0.0085.
Values may be sent and summed in bfloat16 or wider, within the bound.
No kernel may reach another device: no remote copies, remote signals or barrier semaphores. Data moves between devices by JAX's collectives and lax.ppermute only.
A program may use at most 128 MiB of HBM per device.

```python
import math
import jax
import jax.numpy as jnp
from jax import lax

BS = 128
SKETCH = 256
NNZ_DEV = 224
ROWB = 16
COLB = 64
NV = 65536
N_ROW = 32
N_COL = 8


def slot_table(key, local, total):

    def one_device(sub):
        first, second = jax.random.split(sub)
        head = jax.random.permutation(first, local).astype(jnp.int32)
        tail = jax.random.randint(second, (total - local,), 0, local).astype(jnp.int32)
        return jnp.concatenate([head, tail])
    keys = jax.random.split(key, N_ROW * N_COL)
    return jax.vmap(one_device)(keys).reshape(N_ROW, N_COL, total)


def draw_block_rows(key, part):
    key = jax.random.fold_in(key, 11)
    return slot_table(key, ROWB, NNZ_DEV)


def draw_block_cols(key, part):
    key = jax.random.fold_in(key, 23)
    return slot_table(key, COLB, NNZ_DEV)


def draw_live_counts(key, part):
    key = jax.random.fold_in(key, 37)
    first, second = jax.random.split(key)
    lowest = max(ROWB, COLB)
    counts = jax.random.randint(first, (N_ROW * N_COL,), lowest, NNZ_DEV + 1).astype(jnp.int32)
    chosen = jax.random.randint(second, (), 0, N_ROW * N_COL).astype(jnp.int32)
    counts = jnp.where(jnp.arange(N_ROW * N_COL, dtype=jnp.int32) == chosen, NNZ_DEV, counts)
    return counts.astype(jnp.int32).reshape(N_ROW, N_COL)


def draw_row_scale(key, part):
    key = jax.random.fold_in(key, 53)
    position = jnp.arange(NV, dtype=jnp.float32) / NV
    trend = jnp.exp(position * 1.0986)
    rough = jnp.exp(jax.random.uniform(key, (NV,), jnp.float32, -1.0, 1.0))
    return (rough * trend).astype(jnp.float32)


def steps_of(key, extent, shards, least, top_value):
    def one(dim, blocks):
        draws = jax.random.uniform(jax.random.fold_in(jax.random.fold_in(key, 6), dim), (blocks,), jnp.float32, least / len(shards), top_value / len(shards))
        return jnp.repeat(jnp.exp(draws), extent[dim] // blocks).reshape((-1,) + (1,) * (len(extent) - dim - 1))

    factor_of = one(*shards[0])
    for cut in shards[1:]:
        factor_of = factor_of * one(*cut)
    return factor_of


def normal_values(rng, extent, scale, bound, pieces=(), kind=jnp.bfloat16):
    array = jax.random.normal(rng, extent, jnp.float32) * scale
    if len(pieces) > 0:
        array = steps_of(rng, extent, pieces, -0.22, 0.18) * array
    return jnp.clip(array, min=-bound, max=bound).astype(kind)


def setup_inputs(seed: int = 0) -> dict:
    key_list = jax.random.split(jax.random.key(seed), 7)
    return {
        "blocks": normal_values(key_list[0], (N_ROW, N_COL, NNZ_DEV, BS, BS), (BS * NNZ_DEV // ROWB) ** -0.5, 0.125, ((0, 32), (1, 8))),
        "block_rows": draw_block_rows(jax.random.fold_in(key_list[6], 71), 0),
        "block_cols": draw_block_cols(jax.random.fold_in(key_list[6], 71), 0),
        "live_counts": draw_live_counts(jax.random.fold_in(key_list[6], 71), 0),
        "omega": normal_values(key_list[4], (NV, SKETCH), 1.0, 6.0, ((0, 256),)),
        "row_scale": draw_row_scale(jax.random.fold_in(key_list[6], 71), 0),
    }


def device_partial(blk, rows, cols, count, omega_blocks):
    chosen = jnp.take(omega_blocks, cols, axis=0)
    products = jnp.einsum('nij,njk->nik', blk.astype(jnp.float32), chosen.astype(jnp.float32), precision=lax.Precision.HIGHEST)
    live = jnp.arange(NNZ_DEV, dtype=jnp.int32) < count
    onehot = ((rows[None, :] == jnp.arange(ROWB, dtype=jnp.int32)[:, None]) & live[None, :]).astype(jnp.float32)
    summed = jnp.einsum('rn,nik->rik', onehot, products, precision=lax.Precision.HIGHEST)
    return summed.reshape(ROWB * BS, SKETCH)

def reference(blocks, block_rows, block_cols, live_counts, omega, row_scale):
    omega_cols = omega.reshape(N_COL, COLB, BS, SKETCH)

    def per_row(r_index):

        def step(total, c_index):
            part = device_partial(blocks[r_index, c_index], block_rows[r_index, c_index], block_cols[r_index, c_index], live_counts[r_index, c_index], omega_cols[c_index])
            return (total + part, None)
        start = jnp.zeros((ROWB * BS, SKETCH), jnp.float32)
        total, unused = lax.scan(step, start, jnp.arange(N_COL, dtype=jnp.int32))
        return total
    sketch = lax.map(per_row, jnp.arange(N_ROW, dtype=jnp.int32)).reshape(NV, SKETCH)
    sketch = sketch * row_scale[:, None]
    gram = jnp.dot(sketch.T.astype(jnp.float32), sketch.astype(jnp.float32), precision=lax.Precision.HIGHEST, preferred_element_type=jnp.float32)
    lower = jnp.linalg.cholesky(gram)
    solved = jax.scipy.linalg.solve_triangular(lower, sketch.T, lower=True)
    basis = solved.T * math.sqrt(NV)
    factor = lower.T / math.sqrt(NV)
    return (basis, factor)
```

```python
import math

import jax
import jax.numpy as jnp
from jax import lax
from jax.experimental import pallas as pl
from jax.experimental.pallas import tpu as pltpu
from jax.sharding import Mesh
from jax.sharding import PartitionSpec as P

f32 = jnp.float32
HIGHEST = lax.Precision.HIGHEST
BS = 128
GROUP = 16
SIZES = {"z": 8, "y": 4, "x": 4, "core": 2}


def shift(value, axis, step):
    size = SIZES[axis]
    return lax.ppermute(value, axis, [(i, (i + step) % size) for i in range(size)])


def spmm_kernel(rows_ref, cols_ref, count_ref, omega_ref, blocks_ref, out_ref, acc_ref):
    step = pl.program_id(0)
    spare = acc_ref.shape[0] - BS

    @pl.when(step == 0)
    def _():
        acc_ref[...] = jnp.zeros_like(acc_ref)

    @pl.when(step * GROUP < count_ref[0])
    def _():
        for index in range(GROUP):
            slot = step * GROUP + index
            row = jnp.where(slot < count_ref[0], rows_ref[slot] * BS, spare)
            row = pl.multiple_of(row, BS)
            col = pl.multiple_of(cols_ref[slot] * BS, BS)
            product = jnp.dot(
                blocks_ref[index], omega_ref[pl.ds(col, BS), :], preferred_element_type=f32
            )
            acc_ref[pl.ds(row, BS), :] += product

    @pl.when(step == pl.num_programs(0) - 1)
    def _():
        out_ref[...] = acc_ref[pl.ds(0, spare), :]


def spmm(rows, cols, count, omega, blocks, row_blocks):
    slots = blocks.shape[0]
    width = omega.shape[1]
    total = row_blocks * BS

    def group_of(step, rows_ref, cols_ref, count_ref):
        return (jnp.minimum(step, (count_ref[0] - 1) // GROUP), 0, 0)

    return pl.pallas_call(
        spmm_kernel,
        grid_spec=pltpu.PrefetchScalarGridSpec(
            num_scalar_prefetch=3,
            grid=(slots // GROUP,),
            in_specs=[
                pl.BlockSpec(omega.shape, lambda *_: (0, 0)),
                pl.BlockSpec((GROUP, BS, BS), group_of),
            ],
            out_specs=pl.BlockSpec((total, width), lambda *_: (0, 0)),
            scratch_shapes=[pltpu.VMEM((total + BS, width), f32)],
        ),
        out_shape=jax.ShapeDtypeStruct((total, width), f32),
        compiler_params=pltpu.CompilerParams(
            dimension_semantics=("arbitrary",), vmem_limit_bytes=40 * 1024 * 1024
        ),
        name="spmm",
    )(rows, cols, count, omega, blocks)


def dot(a, b, contract):
    return lax.dot_general(
        a, b, ((contract[:1], contract[1:]), ((), ())),
        precision=HIGHEST, preferred_element_type=f32,
    )


def eliminate(sym):
    size = sym.shape[0]
    tiles = size // 8
    lane = lax.broadcasted_iota(jnp.int32, (8, size), 1)
    sub = lax.broadcasted_iota(jnp.int32, (8, size), 0)
    upper = [sym[8 * t:8 * t + 8, :] for t in range(tiles)]
    inverse = [(lane == sub + 8 * t).astype(f32) for t in range(tiles)]
    for k in range(size):
        t, j = divmod(k, 8)
        pivot = 1.0 / upper[t][j:j + 1, k:k + 1]
        row = jnp.broadcast_to(upper[t][j:j + 1, :] * pivot, (8, size))
        row_inverse = jnp.broadcast_to(inverse[t][j:j + 1, :] * pivot, (8, size))
        for i in range(t, tiles):
            if i == t and j == 7:
                continue
            column = jnp.broadcast_to(upper[i][:, k:k + 1], (8, size))
            if i == t:
                column = jnp.where(sub > j, column, 0.0)
            upper[i] = upper[i] - column * row
            inverse[i] = inverse[i] - column * row_inverse
    for t in range(tiles):
        diagonal = jnp.sum(jnp.where(lane == sub + 8 * t, upper[t], 0.0), axis=1, keepdims=True)
        scale = 1.0 / jnp.sqrt(diagonal)
        upper[t] = jnp.where(lane >= sub + 8 * t, upper[t] * scale, 0.0)
        inverse[t] = inverse[t] * scale
    return jnp.concatenate(upper, 0), jnp.concatenate(inverse, 0)


def factor_kernel(gram_ref, sketch_ref, factor_ref, basis_ref, *, scale):
    half = gram_ref.shape[0] // 2
    top, bottom = pl.ds(0, half), pl.ds(half, half)
    upper1, inverse1 = eliminate(gram_ref[top, top])
    cross = dot(inverse1, gram_ref[top, bottom], (1, 0))
    upper2, inverse2 = eliminate(gram_ref[bottom, bottom] - dot(cross, cross, (0, 0)))
    factor_ref[top, top] = upper1 * (1.0 / scale)
    factor_ref[top, bottom] = cross * (1.0 / scale)
    factor_ref[bottom, top] = jnp.zeros((half, half), f32)
    factor_ref[bottom, bottom] = upper2 * (1.0 / scale)
    first = dot(sketch_ref[:, top], inverse1, (1, 1))
    rest = sketch_ref[:, bottom] - dot(first, cross, (1, 0))
    basis_ref[:, top] = first * scale
    basis_ref[:, bottom] = dot(rest, inverse2, (1, 1)) * scale


def orthonormalize(gram, sketch, vertex_total):
    return pl.pallas_call(
        lambda *refs: factor_kernel(*refs, scale=math.sqrt(vertex_total)),
        out_shape=(
            jax.ShapeDtypeStruct(gram.shape, f32),
            jax.ShapeDtypeStruct(sketch.shape, f32),
        ),
        compiler_params=pltpu.CompilerParams(vmem_limit_bytes=32 * 1024 * 1024),
        name="orthonormalize",
    )(gram, sketch)


def spread(value, axes, count):
    copies = jnp.broadcast_to(value[None], (count,) + value.shape)
    return lax.all_to_all(copies, axes, 0, 0, tiled=True)


def sum_over_all(gram):
    rows, width = gram.shape
    pieces = gram.reshape(16, rows // 16, width)
    part = lax.all_to_all(pieces, ("y", "x"), 0, 0, tiled=True).sum(0)
    part = spread(part, ("z", "core"), 16).sum(0)
    return spread(part, ("y", "x"), 16).reshape(rows, width)


def shards(blocks, block_rows, block_cols, live_counts, omega, row_scale):
    own_rows, width = omega.shape
    row_blocks = own_rows * 8 // BS
    per = own_rows // BS
    x_here, core_here = lax.axis_index("x"), lax.axis_index("core")
    rows = block_rows[0, 0]
    x_of, core_of, rest = rows // (2 * per), (rows // per) % 2, rows % per
    rows = (
        jnp.where(core_of == core_here, 4 * per, 0) + ((x_of - x_here + 4) % 4) * per + rest
    )
    gathered = lax.all_gather(omega, ("z", "y"), axis=0, tiled=True)
    partial_sum = spmm(rows, block_cols[0, 0], live_counts[0], gathered, blocks[0, 0], row_blocks)
    theirs, ours = partial_sum[:4 * own_rows], partial_sum[4 * own_rows:]
    ours = ours + shift(theirs, "core", 1)
    pieces = ours.reshape(4, own_rows, width)
    arrived = [shift(pieces[k], "x", k) for k in (1, 3, 2)]
    sketch = pieces[0] + arrived[0] + arrived[1] + arrived[2]
    sketch = sketch * row_scale[:, None]
    gram = sum_over_all(dot(sketch, sketch, (0, 0)))
    factor, basis = orthonormalize(gram, sketch, own_rows * 256)
    return (basis, factor)


def solution(mesh):
    fine = Mesh(mesh.devices.reshape(8, 4, 4, 2), ("z", "y", "x", "core"))
    row, col = ("z", "y"), ("x", "core")
    placed = (
        P(row, col, None, None, None),
        P(row, col, None),
        P(row, col, None),
        P(row, col),
        P(col + row, None),
        P(row + col),
    )
    return jax.shard_map(
        shards,
        mesh=fine,
        in_specs=placed,
        out_specs=(P(row + col, None), P()),
        check_vma=False,
    )
```

```python
import math

import jax
import jax.numpy as jnp
from jax import lax
from jax.experimental import pallas as pl
from jax.experimental.pallas import tpu as pltpu
from jax.sharding import Mesh
from jax.sharding import PartitionSpec as P

f32 = jnp.float32
HIGHEST = lax.Precision.HIGHEST
BS = 128
GROUP = 16
CHUNKS = 7
KIND = 1 << 20
FIRST_LIMIT = 48
SIZES = {"z": 8, "y": 4, "x": 4, "core": 2}


def shift(value, axis, step):
    size = SIZES[axis]
    return lax.ppermute(value, axis, [(i, (i + step) % size) for i in range(size)])


def add_groups(groups, end, list_ref, blocks_ref, omega_ref, out_ref):
    spare = (out_ref.shape[0] // BS - 1) * 256

    def group(step, carry):
        for index in range(GROUP):
            place = step * GROUP + index
            entry = jnp.where(place < end, list_ref[place], spare)
            row = pl.multiple_of((entry // 256) % 32 * BS, BS)
            out_ref[pl.ds(row, BS), :] += jnp.dot(
                blocks_ref[entry % 256], omega_ref[entry // 8192], preferred_element_type=f32
            )
        return carry

    lax.fori_loop(*groups, group, 0)


def copies_of(part_refs, places, omega_ref, sems):
    return [
        pltpu.make_async_copy(part_refs[index], omega_ref.at[pl.ds(*place)], sems.at[index])
        for index, place in enumerate(places)
    ]


def first_kernel(entries_ref, *refs, places):
    part_refs = refs[:len(places)]
    source_ref, out_ref, blocks_ref, late_ref, late_count_ref = refs[len(places):-4]
    early_ref, omega_ref, sems, block_sems = refs[-4:]
    slots = blocks_ref.shape[0]
    chunk = slots // CHUNKS
    loads = [
        pltpu.make_async_copy(
            source_ref.at[pl.ds(i * chunk, chunk)],
            blocks_ref.at[pl.ds(i * chunk, chunk)],
            block_sems.at[i],
        )
        for i in range(CHUNKS)
    ]
    copies = copies_of(part_refs, places, omega_ref, sems)
    for copy in loads[:1] + copies + loads[1:]:
        copy.start()
    out_ref[...] = jnp.zeros_like(out_ref)

    def sort(slot, counts):
        early, late = counts
        entry = entries_ref[slot]
        kind = entry // KIND
        early_ref[early] = entry
        late_ref[late] = entry - KIND
        return early + (kind == 0).astype(jnp.int32), late + (kind == 1).astype(jnp.int32)

    counts, ends = (jnp.int32(0), jnp.int32(0)), []
    for i in range(CHUNKS):
        counts = lax.fori_loop(i * chunk, (i + 1) * chunk, sort, counts, unroll=8)
        ends.append(counts[0])
    late_count_ref[0] = counts[1]
    for copy in copies:
        copy.wait()
    done = 0
    for i, copy in enumerate(loads):
        copy.wait()
        full = ends[i] // GROUP if i < CHUNKS - 1 else (ends[i] + GROUP - 1) // GROUP
        add_groups((done, full), ends[i], early_ref, blocks_ref, omega_ref, out_ref)
        done = full


def rest_kernel(late_ref, late_count_ref, *refs, places):
    part_refs = refs[:len(places)]
    out_ref, blocks_ref, theirs_ref, ours_ref, omega_ref, sems = refs[len(places):]
    copies = copies_of(part_refs, places, omega_ref, sems)
    for copy in copies:
        copy.start()
    for copy in copies:
        copy.wait()
    count = late_count_ref[0]
    groups = 0, (count + GROUP - 1) // GROUP
    add_groups(groups, count, late_ref, blocks_ref, omega_ref, out_ref)
    half = theirs_ref.shape[0]
    theirs_ref[...] = out_ref[pl.ds(0, half), :]
    ours_ref[...] = out_ref[pl.ds(half, half), :]


def block_products(entries, early, late, blocks, total):
    slots, width = blocks.shape[0], early[0][0].shape[-1]
    smem, vmem = (pl.BlockSpec(memory_space=space) for space in (pltpu.SMEM, pltpu.VMEM))
    anywhere = pl.BlockSpec(memory_space=pl.ANY)

    def places_of(parts):
        return [place for _, place in parts]

    def omega_scratch(parts):
        held = max(sum(place) for place in places_of(parts))
        return pltpu.VMEM((held, BS, width), jnp.bfloat16)

    def params(mebibytes):
        return pltpu.CompilerParams(vmem_limit_bytes=mebibytes * 1024 * 1024)

    def cost(flops):
        return pl.CostEstimate(flops=flops, bytes_accessed=0, transcendentals=0)

    before, held, late_list, late_count = pl.pallas_call(
        lambda *refs: first_kernel(*refs, places=places_of(early)),
        in_specs=[smem] + [anywhere] * (len(early) + 1),
        out_specs=(vmem, vmem, smem, smem),
        out_shape=(
            pltpu.VMEM((total + BS, width), f32),
            pltpu.VMEM(blocks.shape, blocks.dtype),
            jax.ShapeDtypeStruct((slots + 2 * GROUP,), jnp.int32),
            jax.ShapeDtypeStruct((1,), jnp.int32),
        ),
        scratch_shapes=[
            pltpu.SMEM((slots + 2 * GROUP,), jnp.int32),
            omega_scratch(early),
            pltpu.SemaphoreType.DMA((len(early),)),
            pltpu.SemaphoreType.DMA((CHUNKS,)),
        ],
        compiler_params=params(FIRST_LIMIT),
        cost_estimate=cost(6 * 10**9),
        name="multiply_first",
    )(entries, *(part for part, _ in early), blocks)
    return pl.pallas_call(
        lambda *refs: rest_kernel(*refs, places=places_of(late)),
        in_specs=[smem] * 2 + [anywhere] * len(late) + [vmem] * 2,
        out_specs=(vmem, vmem),
        out_shape=(jax.ShapeDtypeStruct((total // 2, width), f32),) * 2,
        scratch_shapes=[omega_scratch(late), pltpu.SemaphoreType.DMA((len(late),))],
        compiler_params=params(24),
        cost_estimate=cost(10**9),
        name="multiply_rest",
    )(late_list, late_count, *(part for part, _ in late), before, held)


def dot(a, b, contract):
    return lax.dot_general(
        a, b, ((contract[:1], contract[1:]), ((), ())),
        precision=HIGHEST, preferred_element_type=f32,
    )


def eliminate(sym):
    size = sym.shape[0]
    tiles = size // 8
    full = (8, size)
    lane = lax.broadcasted_iota(jnp.int32, full, 1)
    sub = lax.broadcasted_iota(jnp.int32, full, 0)
    upper = [sym[8 * t:8 * t + 8, :] for t in range(tiles)]
    inverse = [(lane == sub + 8 * t).astype(f32) for t in range(tiles)]
    for t in range(tiles):
        k = 8 * t
        rows = [jnp.broadcast_to(upper[t][i:i + 1, :], full) for i in range(8)]
        inv_rows = [jnp.broadcast_to(inverse[t][i:i + 1, :], full) for i in range(8)]
        own = [jnp.broadcast_to(upper[t][:, k + i:k + i + 1], full) for i in range(8)]
        entry = {
            (a, b): jnp.broadcast_to(own[b][a:a + 1, :], full) for a in range(8) for b in range(a, 8)
        }
        columns = {
            i: [jnp.broadcast_to(upper[i][:, k + a:k + a + 1], full) for a in range(8)]
            for i in range(t + 1, tiles)
        }
        recip, ratio = [], {}
        for a in range(8):
            recip.append(1.0 / entry[a, a])
            for b in range(a + 1, 8):
                ratio[a, b] = entry[a, b] * recip[a]
            for b in range(a + 1, 8):
                for c in range(b, 8):
                    entry[b, c] = entry[b, c] - ratio[a, b] * entry[a, c]
                rows[b] = rows[b] - ratio[a, b] * rows[a]
                inv_rows[b] = inv_rows[b] - ratio[a, b] * inv_rows[a]
            if t + 1 < tiles:
                next_columns = columns[t + 1]
                part = next_columns[a] * recip[a]
                for b in range(a + 1, 8):
                    next_columns[b] = next_columns[b] - next_columns[a] * ratio[a, b]
                upper[t + 1] = upper[t + 1] - part * rows[a]
                inverse[t + 1] = inverse[t + 1] - part * inv_rows[a]
        if t + 2 < tiles:
            back = [rows[a] * recip[a] for a in range(8)]
            inv_back = [inv_rows[a] * recip[a] for a in range(8)]
            for a in range(6, -1, -1):
                for b in range(a + 1, 8):
                    back[a] = back[a] - ratio[a, b] * back[b]
                    inv_back[a] = inv_back[a] - ratio[a, b] * inv_back[b]
            for i in range(t + 2, tiles):
                for a in range(7, -1, -1):
                    upper[i] = upper[i] - columns[i][a] * back[a]
                    inverse[i] = inverse[i] - columns[i][a] * inv_back[a]
        pivot = entry[0, 0]
        for a in range(1, 8):
            upper[t] = jnp.where(sub == a, rows[a], upper[t])
            inverse[t] = jnp.where(sub == a, inv_rows[a], inverse[t])
            pivot = jnp.where(sub == a, entry[a, a], pivot)
        scale = 1.0 / jnp.sqrt(pivot)
        upper[t] = jnp.where(lane >= sub + k, upper[t] * scale, 0.0)
        inverse[t] = inverse[t] * scale
    return jnp.concatenate(upper, 0), jnp.concatenate(inverse, 0)


def factor_kernel(gram_ref, sketch_ref, factor_ref, basis_ref, *, scale):
    half = gram_ref.shape[1]
    top, bottom = pl.ds(0, half), pl.ds(half, half)
    upper1, inverse1 = eliminate(gram_ref[top, :])
    cross = dot(inverse1, gram_ref[bottom, :], (1, 0))
    upper2, inverse2 = eliminate(gram_ref[pl.ds(2 * half, half), :] - dot(cross, cross, (0, 0)))
    factor_ref[top, top] = upper1 * (1.0 / scale)
    factor_ref[top, bottom] = cross * (1.0 / scale)
    factor_ref[bottom, top] = jnp.zeros((half, half), f32)
    factor_ref[bottom, bottom] = upper2 * (1.0 / scale)
    first = dot(sketch_ref[:, top], inverse1, (1, 1))
    rest = sketch_ref[:, bottom] - dot(first, cross, (1, 0))
    basis_ref[:, top] = first * scale
    basis_ref[:, bottom] = dot(rest, inverse2, (1, 1)) * scale


def orthonormalize(gram, sketch, vertex_total):
    return pl.pallas_call(
        lambda *refs: factor_kernel(*refs, scale=math.sqrt(vertex_total)),
        out_shape=(
            jax.ShapeDtypeStruct((sketch.shape[1],) * 2, f32),
            jax.ShapeDtypeStruct(sketch.shape, f32),
        ),
        compiler_params=pltpu.CompilerParams(vmem_limit_bytes=32 * 1024 * 1024),
        name="orthonormalize",
    )(gram, sketch)


def spread(value, axes, count):
    copies = jnp.broadcast_to(value[None], (count,) + value.shape)
    return lax.all_to_all(copies, axes, 0, 0, tiled=True)


def sum_over_all(gram):
    half = gram.shape[0] // 2
    packed = jnp.concatenate([gram[:half, :half], gram[:half, half:], gram[half:, half:]], 0)
    pieces = packed.reshape(16, -1, half)
    part = lax.all_to_all(pieces, ("y", "x"), 0, 0, tiled=True).sum(0)
    part = part + shift(part, "core", 1)
    part = spread(part, ("z",), 8).sum(0)
    return spread(part, ("y", "x"), 16).reshape(packed.shape)


def gather(omega):
    half = omega.shape[0] // 2

    def ring(block, axis):
        size = SIZES[axis]
        forth, back, found = block, block, {0: block}
        for step in range(1, size // 2):
            forth, back = shift(forth, axis, 1), shift(back, axis, -1)
            found[size - step], found[step] = forth, back
        return found, forth, back

    def last(forth, back, axis, dim):
        cut = forth.shape[dim] // 2
        return (
            shift(lax.slice_in_dim(forth, 0, cut, axis=dim), axis, 1),
            shift(lax.slice_in_dim(back, cut, 2 * cut, axis=dim), axis, -1),
        )

    first, second = omega[None, :half], omega[None, half:]
    found1, forth1, back1 = ring(first, "y")
    found2, forth2, back2 = ring(second, "z")
    found1[2] = jnp.concatenate(last(forth1, back1, "y", 1), 1)
    found2[4] = jnp.concatenate(last(forth2, back2, "z", 1), 1)
    block1 = jnp.concatenate([found1[i] for i in range(4)], 0)
    block2 = jnp.concatenate([found2[i] for i in range(8)], 0)
    full1, forth1, back1 = ring(block1, "z")
    full2, forth2, back2 = ring(block2, "y")
    end1, end2 = last(forth1, back1, "z", 0), last(forth2, back2, "y", 0)
    early = [(full1[dz], (4 * dz, 4)) for dz in (0, 7, 1, 6, 2, 5, 3)]
    early += [(full2[dy], (32 + 8 * dy, 8)) for dy in (0, 3, 1)]
    late = [(end1[0], (0, 2)), (end1[1], (2, 2)), (end2[0], (4, 4)), (end2[1], (8, 4))]
    return early, late


def shards(blocks, block_rows, block_cols, live_counts, omega, row_scale):
    own_rows, width = omega.shape
    row_blocks = own_rows * 8 // BS
    per = own_rows // BS
    x_here, core_here = lax.axis_index("x"), lax.axis_index("core")
    rows, cols, count = block_rows[0, 0], block_cols[0, 0], live_counts[0, 0]
    x_of, core_of, rest = rows // (2 * per), (rows // per) % 2, rows % per
    rows = (
        jnp.where(core_of == core_here, 4 * per, 0) + ((x_of - x_here + 4) % 4) * per + rest
    )
    z_here, y_here = lax.axis_index("z"), lax.axis_index("y")
    far_z, far_y = (cols // 8 - z_here + 8) % 8, (cols // 2 - y_here + 4) % 4
    is_second = cols % 2
    is_late = jnp.where(is_second == 1, far_y == 2, far_z == 4)
    cols = jnp.where(
        is_late,
        jnp.where(is_second == 1, 4 + far_z, far_y),
        jnp.where(is_second == 1, 32 + 8 * far_y + far_z, 4 * far_z + far_y),
    )
    slot = jnp.arange(rows.shape[0], dtype=jnp.int32)
    kind = jnp.where(slot < count, is_late.astype(jnp.int32), 2)
    entries = slot + 256 * rows + 8192 * cols + KIND * kind
    early, late = gather(omega)
    theirs, ours = block_products(entries, early, late, blocks[0, 0], row_blocks * BS)
    ours = ours + shift(theirs, "core", 1)
    pieces = ours.reshape(4, own_rows, width)
    arrived = [shift(pieces[k], "x", k) for k in (1, 3, 2)]
    sketch = pieces[0] + arrived[0] + arrived[1] + arrived[2]
    sketch = sketch * row_scale[:, None]
    gram = sum_over_all(dot(sketch, sketch, (0, 0)))
    factor, basis = orthonormalize(gram, sketch, own_rows * 256)
    return (basis, factor)


def solution(mesh):
    fine = Mesh(mesh.devices.reshape(8, 4, 4, 2), ("z", "y", "x", "core"))
    row, col = ("z", "y"), ("x", "core")
    placed = (
        P(row, col, None, None, None),
        P(row, col, None),
        P(row, col, None),
        P(row, col),
        P(col + row, None),
        P(row + col),
    )
    return jax.shard_map(
        shards,
        mesh=fine,
        in_specs=placed,
        out_specs=(P(row + col, None), P()),
        check_vma=False,
    )
```

```python
import math

import jax
import jax.numpy as jnp
from jax import lax
from jax.experimental import pallas as pl
from jax.experimental.pallas import tpu as pltpu
from jax.sharding import Mesh
from jax.sharding import PartitionSpec as P

f32 = jnp.float32
HIGHEST = lax.Precision.HIGHEST
BS = 128
GROUP = 16
KIND = 1 << 20
PREPARE_LIMIT = 46
SIZES = {"z": 8, "y": 4, "x": 4, "core": 2}


def shift(value, axis, step):
    size = SIZES[axis]
    return lax.ppermute(value, axis, [(i, (i + step) % size) for i in range(size)])


def add_groups(groups, end, list_ref, blocks_ref, omega_ref, out_ref):
    spare = (out_ref.shape[0] // BS - 1) * 256

    def group(step, carry):
        for index in range(GROUP):
            place = step * GROUP + index
            entry = jnp.where(place < end, list_ref[place], spare)
            row = pl.multiple_of(((entry >> 8) & 31) * BS, BS)
            out_ref[pl.ds(row, BS), :] += jnp.dot(
                blocks_ref[entry & 255], omega_ref[entry >> 13], preferred_element_type=f32
            )
        return carry

    lax.fori_loop(*groups, group, 0)


def copies_of(part_refs, places, omega_ref, sems):
    return [
        pltpu.make_async_copy(part_refs[index], omega_ref.at[pl.ds(*place)], sems.at[index])
        for index, place in enumerate(places)
    ]


def prepare_kernel(entries_ref, source_ref, blocks_ref, early_ref, late_ref, counts_ref, token_ref, sem):
    load = pltpu.make_async_copy(source_ref, blocks_ref, sem)
    load.start()
    token_ref[...] = jnp.zeros_like(token_ref)

    def sort(slot, counts):
        early, late = counts
        entry = entries_ref[slot]
        kind = entry >> 20
        early_ref[early] = entry
        late_ref[late] = entry & (KIND - 1)
        return early + ((kind + 3) >> 2 ^ 1), late + (kind & 1)

    start = jnp.int32(0), jnp.int32(0)
    counts_ref[0], counts_ref[1] = lax.fori_loop(0, blocks_ref.shape[0], sort, start, unroll=8)
    load.wait()


def multiply_kernel(list_ref, counts_ref, *refs, places, first):
    part_refs = refs[:len(places)]
    blocks_ref, omega_ref, sems = refs[len(places)], *refs[-2:]
    copies = copies_of(part_refs, places, omega_ref, sems)
    for copy in copies:
        copy.start()
    if first:
        out_ref = refs[len(places) + 1]
        out_ref[...] = jnp.zeros_like(out_ref)
    else:
        out_ref, theirs_ref, ours_ref, peak_ref = refs[len(places) + 1:-2]
    for copy in copies:
        copy.wait()
    count = counts_ref[0 if first else 1]
    groups = 0, (count + GROUP - 1) // GROUP
    add_groups(groups, count, list_ref, blocks_ref, omega_ref, out_ref)
    if not first:
        half = ours_ref.shape[0]
        theirs, ours = out_ref[pl.ds(0, half), :], out_ref[pl.ds(half, half), :]
        theirs_ref[pl.ds(0, half), :] = theirs
        ours_ref[...] = ours
        for value, ref in ((theirs, theirs_ref.at[pl.ds(half, 8)]), (ours, peak_ref)):
            peak = jnp.max(jnp.abs(value), axis=0, keepdims=True)
            ref[...] = jnp.broadcast_to(peak, ref.shape)


def prepare(entries, blocks):
    smem, vmem = (pl.BlockSpec(memory_space=space) for space in (pltpu.SMEM, pltpu.VMEM))
    listed = jax.ShapeDtypeStruct((blocks.shape[0] + 2 * GROUP,), jnp.int32)
    return pl.pallas_call(
        prepare_kernel,
        in_specs=[smem, pl.BlockSpec(memory_space=pl.ANY)],
        out_specs=(vmem, smem, smem, smem, vmem),
        out_shape=(
            pltpu.VMEM(blocks.shape, blocks.dtype),
            listed,
            listed,
            jax.ShapeDtypeStruct((2,), jnp.int32),
            jax.ShapeDtypeStruct((16, BS), jnp.bfloat16),
        ),
        scratch_shapes=[pltpu.SemaphoreType.DMA(())],
        compiler_params=pltpu.CompilerParams(vmem_limit_bytes=PREPARE_LIMIT * 1024 * 1024),
        cost_estimate=pl.CostEstimate(
            flops=0, bytes_accessed=8 * blocks.size, transcendentals=0
        ),
        name="prepare",
    )(entries, blocks)


def multiply(slots, counts, parts, blocks, total, before=None):
    first, width = before is None, parts[0][0].shape[-1]
    places = [place for _, place in parts]
    smem, vmem = (pl.BlockSpec(memory_space=space) for space in (pltpu.SMEM, pltpu.VMEM))
    if first:
        out_shape = pltpu.VMEM((total + BS, width), f32)
    else:
        out_shape = tuple(
            jax.ShapeDtypeStruct((rows, width), f32) for rows in (total // 2 + 8, total // 2, 8)
        )
    return pl.pallas_call(
        lambda *refs: multiply_kernel(*refs, places=places, first=first),
        in_specs=[smem] * 2
        + [pl.BlockSpec(memory_space=pl.ANY)] * len(parts)
        + [vmem] * (1 if first else 2),
        out_specs=vmem if first else (vmem,) * 3,
        out_shape=out_shape,
        scratch_shapes=[
            pltpu.VMEM((max(sum(place) for place in places), BS, width), jnp.bfloat16),
            pltpu.SemaphoreType.DMA((len(parts),)),
        ],
        compiler_params=pltpu.CompilerParams(vmem_limit_bytes=24 * 1024 * 1024),
        cost_estimate=pl.CostEstimate(
            flops=(6 if first else 1) * 10**9, bytes_accessed=0, transcendentals=0
        ),
        name="multiply_first" if first else "multiply_rest",
    )(slots, counts, *(part for part, _ in parts), blocks, *(() if first else (before,)))


def dot(a, b, contract):
    return lax.dot_general(
        a, b, ((contract[:1], contract[1:]), ((), ())),
        precision=HIGHEST, preferred_element_type=f32,
    )


def eliminate(sym):
    size = sym.shape[0]
    tiles = size // 8
    full = (8, size)
    lane = lax.broadcasted_iota(jnp.int32, full, 1)
    sub = lax.broadcasted_iota(jnp.int32, full, 0)
    upper = [sym[8 * t:8 * t + 8, :] for t in range(tiles)]
    inverse = [(lane == sub + 8 * t).astype(f32) for t in range(tiles)]
    for t in range(tiles):
        k = 8 * t
        rows = [jnp.broadcast_to(upper[t][i:i + 1, :], full) for i in range(8)]
        inv_rows = [jnp.broadcast_to(inverse[t][i:i + 1, :], full) for i in range(8)]
        own = [jnp.broadcast_to(upper[t][:, k + i:k + i + 1], full) for i in range(8)]
        entry = {
            (a, b): jnp.broadcast_to(own[b][a:a + 1, :], full) for a in range(8) for b in range(a, 8)
        }
        columns = {
            i: [jnp.broadcast_to(upper[i][:, k + a:k + a + 1], full) for a in range(8)]
            for i in range(t + 1, tiles)
        }
        recip, ratio = [], {}
        for a in range(8):
            recip.append(1.0 / entry[a, a])
            for b in range(a + 1, 8):
                ratio[a, b] = entry[a, b] * recip[a]
            for b in range(a + 1, 8):
                for c in range(b, 8):
                    entry[b, c] = entry[b, c] - ratio[a, b] * entry[a, c]
                rows[b] = rows[b] - ratio[a, b] * rows[a]
                inv_rows[b] = inv_rows[b] - ratio[a, b] * inv_rows[a]
            if t + 1 < tiles:
                next_columns = columns[t + 1]
                part = next_columns[a] * recip[a]
                for b in range(a + 1, 8):
                    next_columns[b] = next_columns[b] - next_columns[a] * ratio[a, b]
                upper[t + 1] = upper[t + 1] - part * rows[a]
                inverse[t + 1] = inverse[t + 1] - part * inv_rows[a]
        if t + 2 < tiles:
            back = [rows[a] * recip[a] for a in range(8)]
            inv_back = [inv_rows[a] * recip[a] for a in range(8)]
            for a in range(6, -1, -1):
                for b in range(a + 1, 8):
                    back[a] = back[a] - ratio[a, b] * back[b]
                    inv_back[a] = inv_back[a] - ratio[a, b] * inv_back[b]
            for i in range(t + 2, tiles):
                for a in range(7, -1, -1):
                    upper[i] = upper[i] - columns[i][a] * back[a]
                    inverse[i] = inverse[i] - columns[i][a] * inv_back[a]
        pivot = entry[0, 0]
        for a in range(1, 8):
            upper[t] = jnp.where(sub == a, rows[a], upper[t])
            inverse[t] = jnp.where(sub == a, inv_rows[a], inverse[t])
            pivot = jnp.where(sub == a, entry[a, a], pivot)
        scale = 1.0 / jnp.sqrt(pivot)
        upper[t] = jnp.where(lane >= sub + k, upper[t] * scale, 0.0)
        inverse[t] = inverse[t] * scale
    return jnp.concatenate(upper, 0), jnp.concatenate(inverse, 0)


def factor_kernel(gram_ref, sketch_ref, factor_ref, basis_ref, *, scale):
    half = gram_ref.shape[1]
    top, bottom = pl.ds(0, half), pl.ds(half, half)
    upper1, inverse1 = eliminate(gram_ref[top, :])
    cross = dot(inverse1, gram_ref[bottom, :], (1, 0))
    upper2, inverse2 = eliminate(gram_ref[pl.ds(2 * half, half), :] - dot(cross, cross, (0, 0)))
    factor_ref[top, top] = upper1 * (1.0 / scale)
    factor_ref[top, bottom] = cross * (1.0 / scale)
    factor_ref[bottom, top] = jnp.zeros((half, half), f32)
    factor_ref[bottom, bottom] = upper2 * (1.0 / scale)
    first = dot(sketch_ref[:, top], inverse1, (1, 1))
    rest = sketch_ref[:, bottom] - dot(first, cross, (1, 0))
    basis_ref[:, top] = first * scale
    basis_ref[:, bottom] = dot(rest, inverse2, (1, 1)) * scale


def orthonormalize(gram, sketch, vertex_total):
    return pl.pallas_call(
        lambda *refs: factor_kernel(*refs, scale=math.sqrt(vertex_total)),
        out_shape=(
            jax.ShapeDtypeStruct((sketch.shape[1],) * 2, f32),
            jax.ShapeDtypeStruct(sketch.shape, f32),
        ),
        compiler_params=pltpu.CompilerParams(vmem_limit_bytes=32 * 1024 * 1024),
        name="orthonormalize",
    )(gram, sketch)


def spread(value, axes, count):
    copies = jnp.broadcast_to(value[None], (count,) + value.shape)
    return lax.all_to_all(copies, axes, 0, 0, tiled=True)


def sum_over_all(gram):
    half = gram.shape[0] // 2
    packed = jnp.concatenate([gram[:half, :half], gram[:half, half:], gram[half:, half:]], 0)
    pieces = packed.reshape(16, -1, half)
    part = lax.all_to_all(pieces, ("y", "x"), 0, 0, tiled=True).sum(0)
    part = part + shift(part, "core", 1)
    part = spread(part, ("z",), 8).sum(0)
    return spread(part, ("y", "x"), 16).reshape(packed.shape)


def split_shift(value, axis):
    size = SIZES[axis]
    pairs = []
    for i in range(size):
        pairs += [(2 * i, 2 * ((i + 1) % size)), (2 * i + 1, 2 * ((i - 1) % size) + 1)]
    return lax.ppermute(value, (axis, "core"), pairs)


def gather(omega, token):
    half = omega.shape[0] // 2

    def short_way(both, axis):
        count = SIZES[axis] // 2
        steps = [both]
        for _ in range(count - 1):
            steps.append(split_shift(steps[-1], axis))
        end = split_shift(steps[-1][:1], axis)
        others = shift(jnp.concatenate([step[1:] for step in steps[1:]], 0), "core", 1)
        near = [step[:1] for step in steps]
        return jnp.concatenate([near[0], others, end] + near[:0:-1], 0)

    def ring(block, axis, token=None):
        size = SIZES[axis]
        forth, back, found = block, block, {0: block}
        for step in range(1, size // 2):
            forth, back = shift(forth, axis, 1), shift(back, axis, -1)
            if step == 1 and token is not None:
                forth, token = lax.optimization_barrier((forth, token))
            found[size - step], found[step] = forth, back
        return found, forth, back

    def last(forth, back, axis):
        cut = forth.shape[0] // 2
        return shift(forth[:cut], axis, 1), shift(back[cut:], axis, -1)

    both = jnp.stack([omega, shift(omega, "core", 1)])
    block1, block2 = short_way(both[:, :half], "y"), short_way(both[:, half:], "z")
    full1, forth1, back1 = ring(block1, "z", token)
    full2, forth2, back2 = ring(block2, "y")
    end1, end2 = last(forth1, back1, "z"), last(forth2, back2, "y")
    early = [(full1[dz], (4 * dz, 4)) for dz in (0, 7, 1, 6, 2, 5, 3)]
    early += [(full2[dy], (32 + 8 * dy, 8)) for dy in (0, 3, 1)]
    late = [(end1[0], (0, 2)), (end1[1], (2, 2)), (end2[0], (4, 4)), (end2[1], (8, 4))]
    return early, late


def sum_over_columns(theirs, ours, peak):
    received = shift(theirs, "core", 1)
    count = ours.shape[0]
    ours = ours + received[:count]
    rows = count // 4
    bound = jnp.maximum(peak[:1] + received[count:count + 1], 1e-30)
    exponent = jnp.ceil(jnp.log2(bound)) - 13.0
    sent = ours[rows:] * jnp.exp2(-exponent)
    exponents = jnp.broadcast_to(exponent, (16, exponent.shape[1]))
    result = ours[:rows]
    for k in (2, 1, 3):
        term = jnp.concatenate([sent[(k - 1) * rows:k * rows], exponents], 0)
        term = shift(term.astype(jnp.float16), "x", k).astype(f32)
        result = result + term[:rows] * jnp.exp2(term[rows:rows + 1])
    return result


def shards(blocks, block_rows, block_cols, live_counts, omega, row_scale):
    own_rows, width = omega.shape
    row_blocks = own_rows * 8 // BS
    per = own_rows // BS
    x_here, core_here = lax.axis_index("x"), lax.axis_index("core")
    rows, cols, count = block_rows[0, 0], block_cols[0, 0], live_counts[0, 0]
    x_of, core_of, rest = rows // (2 * per), (rows // per) % 2, rows % per
    rows = (
        jnp.where(core_of == core_here, 4 * per, 0) + ((x_of - x_here + 4) % 4) * per + rest
    )
    z_here, y_here = lax.axis_index("z"), lax.axis_index("y")
    far_z, far_y = (cols // 8 - z_here + 8) % 8, (cols // 2 - y_here + 4) % 4
    is_second = cols % 2
    is_late = jnp.where(is_second == 1, far_y == 2, far_z == 4)
    back = core_here == 1
    far_z = jnp.where(back & (is_second == 1), (8 - far_z) % 8, far_z)
    far_y = jnp.where(back & (is_second == 0), (4 - far_y) % 4, far_y)
    cols = jnp.where(
        is_late,
        jnp.where(is_second == 1, 4 + far_z, far_y),
        jnp.where(is_second == 1, 32 + 8 * far_y + far_z, 4 * far_z + far_y),
    )
    slot = jnp.arange(rows.shape[0], dtype=jnp.int32)
    kind = jnp.where(slot < count, is_late.astype(jnp.int32), 2)
    entries = slot + 256 * rows + 8192 * cols + KIND * kind
    held, early_list, late_list, counts, token = prepare(entries, blocks[0, 0])
    early, late = gather(omega, token)
    total = row_blocks * BS
    before = multiply(early_list, counts, early, held, total)
    theirs, ours, peak = multiply(late_list, counts, late, held, total, before)
    sketch = sum_over_columns(theirs, ours, peak)
    sketch = sketch * row_scale[:, None]
    gram = sum_over_all(dot(sketch, sketch, (0, 0)))
    factor, basis = orthonormalize(gram, sketch, own_rows * 256)
    return (basis, factor)


def solution(mesh):
    fine = Mesh(mesh.devices.reshape(8, 4, 4, 2), ("z", "y", "x", "core"))
    row, col = ("z", "y"), ("x", "core")
    placed = (
        P(row, col, None, None, None),
        P(row, col, None),
        P(row, col, None),
        P(row, col),
        P(col + row, None),
        P(row + col),
    )
    return jax.shard_map(
        shards,
        mesh=fine,
        in_specs=placed,
        out_specs=(P(row + col, None), P()),
        check_vma=False,
    )
```

```python
import math

import jax
import jax.numpy as jnp
from jax import lax
from jax.experimental import pallas as pl
from jax.experimental.pallas import tpu as pltpu
from jax.sharding import Mesh
from jax.sharding import PartitionSpec as P

f32 = jnp.float32
HIGHEST = lax.Precision.HIGHEST
BS = 128
GROUP = 16
KIND = 1 << 20
PREPARE_LIMIT = 46
SIZES = {"z": 8, "y": 4, "x": 4, "core": 2}


def shift(value, axis, step):
    size = SIZES[axis]
    return lax.ppermute(value, axis, [(i, (i + step) % size) for i in range(size)])


def add_groups(groups, end, list_ref, blocks_ref, omega_ref, out_ref):
    spare = (out_ref.shape[0] // BS - 1) * 256

    def group(step, carry):
        for index in range(GROUP):
            place = step * GROUP + index
            entry = jnp.where(place < end, list_ref[place], spare)
            row = pl.multiple_of(((entry >> 8) & 31) * BS, BS)
            out_ref[pl.ds(row, BS), :] += jnp.dot(
                blocks_ref[entry & 255], omega_ref[entry >> 13], preferred_element_type=f32
            )
        return carry

    lax.fori_loop(*groups, group, 0)


def copies_of(part_refs, places, omega_ref, sems):
    return [
        pltpu.make_async_copy(part_refs[index], omega_ref.at[pl.ds(*place)], sems.at[index])
        for index, place in enumerate(places)
    ]


def prepare_kernel(entries_ref, source_ref, blocks_ref, early_ref, late_ref, counts_ref, token_ref, sem):
    load = pltpu.make_async_copy(source_ref, blocks_ref, sem)
    load.start()
    token_ref[...] = jnp.zeros_like(token_ref)

    def sort(slot, counts):
        early, late = counts
        entry = entries_ref[slot]
        kind = entry >> 20
        early_ref[early] = entry
        late_ref[late] = entry & (KIND - 1)
        return early + ((kind + 3) >> 2 ^ 1), late + (kind & 1)

    start = jnp.int32(0), jnp.int32(0)
    counts_ref[0], counts_ref[1] = lax.fori_loop(0, blocks_ref.shape[0], sort, start, unroll=8)
    load.wait()


def multiply_kernel(list_ref, counts_ref, *refs, places, first):
    part_refs = refs[:len(places)]
    blocks_ref, omega_ref, sems = refs[len(places)], *refs[-2:]
    copies = copies_of(part_refs, places, omega_ref, sems)
    for copy in copies:
        copy.start()
    if first:
        out_ref = refs[len(places) + 1]
        out_ref[...] = jnp.zeros_like(out_ref)
    else:
        out_ref, theirs_ref, ours_ref, peak_ref = refs[len(places) + 1:-2]
    for copy in copies:
        copy.wait()
    count = counts_ref[0 if first else 1]
    groups = 0, (count + GROUP - 1) // GROUP
    add_groups(groups, count, list_ref, blocks_ref, omega_ref, out_ref)
    if not first:
        half = ours_ref.shape[0]
        theirs, ours = out_ref[pl.ds(0, half), :], out_ref[pl.ds(half, half), :]
        theirs_ref[pl.ds(0, half), :] = theirs
        ours_ref[...] = ours
        for value, ref in ((theirs, theirs_ref.at[pl.ds(half, 8)]), (ours, peak_ref)):
            peak = jnp.max(jnp.abs(value), axis=0, keepdims=True)
            ref[...] = jnp.broadcast_to(peak, ref.shape)


def prepare(entries, blocks):
    smem, vmem = (pl.BlockSpec(memory_space=space) for space in (pltpu.SMEM, pltpu.VMEM))
    listed = jax.ShapeDtypeStruct((blocks.shape[0] + 2 * GROUP,), jnp.int32)
    return pl.pallas_call(
        prepare_kernel,
        in_specs=[smem, pl.BlockSpec(memory_space=pl.ANY)],
        out_specs=(vmem, smem, smem, smem, vmem),
        out_shape=(
            pltpu.VMEM(blocks.shape, blocks.dtype),
            listed,
            listed,
            jax.ShapeDtypeStruct((2,), jnp.int32),
            jax.ShapeDtypeStruct((16, BS), jnp.bfloat16),
        ),
        scratch_shapes=[pltpu.SemaphoreType.DMA(())],
        compiler_params=pltpu.CompilerParams(vmem_limit_bytes=PREPARE_LIMIT * 1024 * 1024),
        cost_estimate=pl.CostEstimate(
            flops=0, bytes_accessed=8 * blocks.size, transcendentals=0
        ),
        name="prepare",
    )(entries, blocks)


def multiply(slots, counts, parts, blocks, total, before=None):
    first, width = before is None, parts[0][0].shape[-1]
    places = [place for _, place in parts]
    smem, vmem = (pl.BlockSpec(memory_space=space) for space in (pltpu.SMEM, pltpu.VMEM))
    if first:
        out_shape = pltpu.VMEM((total + BS, width), f32)
    else:
        out_shape = tuple(
            jax.ShapeDtypeStruct((rows, width), f32) for rows in (total // 2 + 8, total // 2, 8)
        )
    return pl.pallas_call(
        lambda *refs: multiply_kernel(*refs, places=places, first=first),
        in_specs=[smem] * 2
        + [pl.BlockSpec(memory_space=pl.ANY)] * len(parts)
        + [vmem] * (1 if first else 2),
        out_specs=vmem if first else (vmem,) * 3,
        out_shape=out_shape,
        scratch_shapes=[
            pltpu.VMEM((max(sum(place) for place in places), BS, width), jnp.bfloat16),
            pltpu.SemaphoreType.DMA((len(parts),)),
        ],
        compiler_params=pltpu.CompilerParams(vmem_limit_bytes=24 * 1024 * 1024),
        cost_estimate=pl.CostEstimate(
            flops=(6 if first else 1) * 10**9, bytes_accessed=0, transcendentals=0
        ),
        name="multiply_first" if first else "multiply_rest",
    )(slots, counts, *(part for part, _ in parts), blocks, *(() if first else (before,)))


def dot(a, b, contract):
    return lax.dot_general(
        a, b, ((contract[:1], contract[1:]), ((), ())),
        precision=HIGHEST, preferred_element_type=f32,
    )


def eliminate(sym):
    size = sym.shape[0]
    tiles = size // 8
    full = (8, size)
    lane = lax.broadcasted_iota(jnp.int32, full, 1)
    sub = lax.broadcasted_iota(jnp.int32, full, 0)
    upper = [sym[8 * t:8 * t + 8, :] for t in range(tiles)]
    inverse = [(lane == sub + 8 * t).astype(f32) for t in range(tiles)]
    for t in range(tiles):
        k = 8 * t
        rows = [jnp.broadcast_to(upper[t][i:i + 1, :], full) for i in range(8)]
        inv_rows = [jnp.broadcast_to(inverse[t][i:i + 1, :], full) for i in range(8)]
        own = [jnp.broadcast_to(upper[t][:, k + i:k + i + 1], full) for i in range(8)]
        entry = {
            (a, b): jnp.broadcast_to(own[b][a:a + 1, :], full) for a in range(8) for b in range(a, 8)
        }
        columns = {
            i: [jnp.broadcast_to(upper[i][:, k + a:k + a + 1], full) for a in range(8)]
            for i in range(t + 1, tiles)
        }
        recip, ratio = [], {}
        for a in range(8):
            recip.append(1.0 / entry[a, a])
            for b in range(a + 1, 8):
                ratio[a, b] = entry[a, b] * recip[a]
            for b in range(a + 1, 8):
                for c in range(b, 8):
                    entry[b, c] = entry[b, c] - ratio[a, b] * entry[a, c]
                rows[b] = rows[b] - ratio[a, b] * rows[a]
                inv_rows[b] = inv_rows[b] - ratio[a, b] * inv_rows[a]
            if t + 1 < tiles:
                next_columns = columns[t + 1]
                part = next_columns[a] * recip[a]
                for b in range(a + 1, 8):
                    next_columns[b] = next_columns[b] - next_columns[a] * ratio[a, b]
                upper[t + 1] = upper[t + 1] - part * rows[a]
                inverse[t + 1] = inverse[t + 1] - part * inv_rows[a]
        if t + 2 < tiles:
            back = [rows[a] * recip[a] for a in range(8)]
            inv_back = [inv_rows[a] * recip[a] for a in range(8)]
            for a in range(6, -1, -1):
                for b in range(a + 1, 8):
                    back[a] = back[a] - ratio[a, b] * back[b]
                    inv_back[a] = inv_back[a] - ratio[a, b] * inv_back[b]
            for i in range(t + 2, tiles):
                for a in range(7, -1, -1):
                    upper[i] = upper[i] - columns[i][a] * back[a]
                    inverse[i] = inverse[i] - columns[i][a] * inv_back[a]
        pivot = entry[0, 0]
        for a in range(1, 8):
            upper[t] = jnp.where(sub == a, rows[a], upper[t])
            inverse[t] = jnp.where(sub == a, inv_rows[a], inverse[t])
            pivot = jnp.where(sub == a, entry[a, a], pivot)
        scale = 1.0 / jnp.sqrt(pivot)
        upper[t] = jnp.where(lane >= sub + k, upper[t] * scale, 0.0)
        inverse[t] = inverse[t] * scale
    return jnp.concatenate(upper, 0), jnp.concatenate(inverse, 0)


def factor_kernel(gram_ref, sketch_ref, factor_ref, basis_ref, *, scale):
    half = gram_ref.shape[1]
    top, bottom = pl.ds(0, half), pl.ds(half, half)
    upper1, inverse1 = eliminate(gram_ref[top, :])
    cross = dot(inverse1, gram_ref[bottom, :], (1, 0))
    upper2, inverse2 = eliminate(gram_ref[pl.ds(2 * half, half), :] - dot(cross, cross, (0, 0)))
    factor_ref[top, top] = upper1 * (1.0 / scale)
    factor_ref[top, bottom] = cross * (1.0 / scale)
    factor_ref[bottom, top] = jnp.zeros((half, half), f32)
    factor_ref[bottom, bottom] = upper2 * (1.0 / scale)
    first = dot(sketch_ref[:, top], inverse1, (1, 1))
    rest = sketch_ref[:, bottom] - dot(first, cross, (1, 0))
    basis_ref[:, top] = first * scale
    basis_ref[:, bottom] = dot(rest, inverse2, (1, 1)) * scale


def orthonormalize(gram, sketch, vertex_total):
    return pl.pallas_call(
        lambda *refs: factor_kernel(*refs, scale=math.sqrt(vertex_total)),
        out_shape=(
            jax.ShapeDtypeStruct((sketch.shape[1],) * 2, f32),
            jax.ShapeDtypeStruct(sketch.shape, f32),
        ),
        compiler_params=pltpu.CompilerParams(vmem_limit_bytes=32 * 1024 * 1024),
        name="orthonormalize",
    )(gram, sketch)


def spread(value, axes, count):
    copies = jnp.broadcast_to(value[None], (count,) + value.shape)
    return lax.all_to_all(copies, axes, 0, 0, tiled=True)


def sum_over_all(gram):
    half = gram.shape[0] // 2
    packed = jnp.concatenate([gram[:half, :half], gram[:half, half:], gram[half:, half:]], 0)
    pieces = packed.reshape(16, -1, half)
    part = lax.all_to_all(pieces, ("y", "x"), 0, 0, tiled=True).sum(0)
    part = part + shift(part, "core", 1)
    part = spread(part, ("z",), 8).sum(0)
    return spread(part, ("y", "x"), 16).reshape(packed.shape)


def split_shift(value, axis):
    size = SIZES[axis]
    pairs = []
    for i in range(size):
        pairs += [(2 * i, 2 * ((i + 1) % size)), (2 * i + 1, 2 * ((i - 1) % size) + 1)]
    return lax.ppermute(value, (axis, "core"), pairs)


def gather(omega, token):
    half = omega.shape[0] // 2

    def short_way(both, axis):
        count = SIZES[axis] // 2
        steps = [both]
        for _ in range(count - 1):
            steps.append(split_shift(steps[-1], axis))
        end = split_shift(steps[-1][:1], axis)
        others = shift(jnp.concatenate([step[1:] for step in steps[1:]], 0), "core", 1)
        near = [step[:1] for step in steps]
        return jnp.concatenate([near[0], others, end] + near[:0:-1], 0)

    def ring(block, axis, token=None):
        size = SIZES[axis]
        forth, back, found = block, block, {0: block}
        for step in range(1, size // 2):
            forth, back = shift(forth, axis, 1), shift(back, axis, -1)
            if step == 1 and token is not None:
                forth, token = lax.optimization_barrier((forth, token))
            found[size - step], found[step] = forth, back
        return found, forth, back

    def last(forth, back, axis):
        cut = forth.shape[0] // 2
        return shift(forth[:cut], axis, 1), shift(back[cut:], axis, -1)

    both = jnp.stack([omega, shift(omega, "core", 1)])
    block1, block2 = short_way(both[:, :half], "y"), short_way(both[:, half:], "z")
    full1, forth1, back1 = ring(block1, "z")
    block2, token = lax.optimization_barrier((block2, token))
    full2, forth2, back2 = ring(block2, "y")
    end1, end2 = last(forth1, back1, "z"), last(forth2, back2, "y")
    early = [(full1[dz], (4 * dz, 4)) for dz in (0, 7, 1, 6, 2, 5, 3)]
    early += [(full2[dy], (32 + 8 * dy, 8)) for dy in (0, 3, 1)]
    late = [(end1[0], (0, 2)), (end1[1], (2, 2)), (end2[0], (4, 4)), (end2[1], (8, 4))]
    return early, late


def sum_over_columns(theirs, ours, peak):
    received = shift(theirs, "core", 1)
    count = ours.shape[0]
    ours = ours + received[:count]
    rows = count // 4
    bound = jnp.maximum(peak[:1] + received[count:count + 1], 1e-30)
    exponent = jnp.ceil(jnp.log2(bound)) - 13.0
    sent = ours[rows:] * jnp.exp2(-exponent)
    exponents = jnp.broadcast_to(exponent, (16, exponent.shape[1]))
    result = ours[:rows]
    for k in (2, 1, 3):
        term = jnp.concatenate([sent[(k - 1) * rows:k * rows], exponents], 0)
        term = shift(term.astype(jnp.float16), "x", k).astype(f32)
        result = result + term[:rows] * jnp.exp2(term[rows:rows + 1])
    return result


def shards(blocks, block_rows, block_cols, live_counts, omega, row_scale):
    own_rows, width = omega.shape
    row_blocks = own_rows * 8 // BS
    per = own_rows // BS
    x_here, core_here = lax.axis_index("x"), lax.axis_index("core")
    rows, cols, count = block_rows[0, 0], block_cols[0, 0], live_counts[0, 0]
    x_of, core_of, rest = rows // (2 * per), (rows // per) % 2, rows % per
    rows = (
        jnp.where(core_of == core_here, 4 * per, 0) + ((x_of - x_here + 4) % 4) * per + rest
    )
    z_here, y_here = lax.axis_index("z"), lax.axis_index("y")
    far_z, far_y = (cols // 8 - z_here + 8) % 8, (cols // 2 - y_here + 4) % 4
    is_second = cols % 2
    is_late = jnp.where(is_second == 1, far_y == 2, far_z == 4)
    back = core_here == 1
    far_z = jnp.where(back & (is_second == 1), (8 - far_z) % 8, far_z)
    far_y = jnp.where(back & (is_second == 0), (4 - far_y) % 4, far_y)
    cols = jnp.where(
        is_late,
        jnp.where(is_second == 1, 4 + far_z, far_y),
        jnp.where(is_second == 1, 32 + 8 * far_y + far_z, 4 * far_z + far_y),
    )
    slot = jnp.arange(rows.shape[0], dtype=jnp.int32)
    kind = jnp.where(slot < count, is_late.astype(jnp.int32), 2)
    entries = slot + 256 * rows + 8192 * cols + KIND * kind
    held, early_list, late_list, counts, token = prepare(entries, blocks[0, 0])
    early, late = gather(omega, token)
    total = row_blocks * BS
    before = multiply(early_list, counts, early, held, total)
    theirs, ours, peak = multiply(late_list, counts, late, held, total, before)
    sketch = sum_over_columns(theirs, ours, peak)
    sketch = sketch * row_scale[:, None]
    gram = sum_over_all(dot(sketch, sketch, (0, 0)))
    factor, basis = orthonormalize(gram, sketch, own_rows * 256)
    return (basis, factor)


def solution(mesh):
    fine = Mesh(mesh.devices.reshape(8, 4, 4, 2), ("z", "y", "x", "core"))
    row, col = ("z", "y"), ("x", "core")
    placed = (
        P(row, col, None, None, None),
        P(row, col, None),
        P(row, col, None),
        P(row, col),
        P(col + row, None),
        P(row + col),
    )
    return jax.shard_map(
        shards,
        mesh=fine,
        in_specs=placed,
        out_specs=(P(row + col, None), P()),
        check_vma=False,
    )
```

```python
import math

import jax
import jax.numpy as jnp
from jax import lax
from jax.experimental import pallas as pl
from jax.experimental.pallas import tpu as pltpu
from jax.sharding import Mesh
from jax.sharding import PartitionSpec as P

f32 = jnp.float32
HIGHEST = lax.Precision.HIGHEST
BS = 128
GROUP = 16
KIND = 1 << 20
PREPARE_LIMIT = 46
SIZES = {"z": 8, "y": 4, "x": 4, "core": 2}


def shift(value, axis, step):
    size = SIZES[axis]
    return lax.ppermute(value, axis, [(i, (i + step) % size) for i in range(size)])


def add_groups(groups, end, list_ref, blocks_ref, omega_ref, out_ref):
    spare = (out_ref.shape[0] // BS - 1) * 256

    def group(step, carry):
        for index in range(GROUP):
            place = step * GROUP + index
            entry = jnp.where(place < end, list_ref[place], spare)
            row = pl.multiple_of(((entry >> 8) & 31) * BS, BS)
            out_ref[pl.ds(row, BS), :] += jnp.dot(
                blocks_ref[entry & 255], omega_ref[entry >> 13], preferred_element_type=f32
            )
        return carry

    lax.fori_loop(*groups, group, 0)


def copies_of(part_refs, places, omega_ref, sems):
    return [
        pltpu.make_async_copy(part_refs[index], omega_ref.at[pl.ds(*place)], sems.at[index])
        for index, place in enumerate(places)
    ]


def prepare_kernel(entries_ref, source_ref, blocks_ref, early_ref, late_ref, counts_ref, token_ref, sem):
    load = pltpu.make_async_copy(source_ref, blocks_ref, sem)
    load.start()
    token_ref[...] = jnp.zeros_like(token_ref)

    def sort(slot, counts):
        early, late = counts
        entry = entries_ref[slot]
        kind = entry >> 20
        early_ref[early] = entry
        late_ref[late] = entry & (KIND - 1)
        return early + ((kind + 3) >> 2 ^ 1), late + (kind & 1)

    start = jnp.int32(0), jnp.int32(0)
    counts_ref[0], counts_ref[1] = lax.fori_loop(0, blocks_ref.shape[0], sort, start, unroll=8)
    load.wait()


def multiply_kernel(list_ref, counts_ref, *refs, places, first):
    part_refs = refs[:len(places)]
    blocks_ref, omega_ref, sems = refs[len(places)], *refs[-2:]
    copies = copies_of(part_refs, places, omega_ref, sems)
    for copy in copies:
        copy.start()
    if first:
        out_ref = refs[len(places) + 1]
        out_ref[...] = jnp.zeros_like(out_ref)
    else:
        out_ref, theirs_ref, ours_ref, peak_ref = refs[len(places) + 1:-2]
    for copy in copies:
        copy.wait()
    count = counts_ref[0 if first else 1]
    groups = 0, (count + GROUP - 1) // GROUP
    add_groups(groups, count, list_ref, blocks_ref, omega_ref, out_ref)
    if not first:
        half = ours_ref.shape[0]
        theirs, ours = out_ref[pl.ds(0, half), :], out_ref[pl.ds(half, half), :]
        theirs_ref[pl.ds(0, half), :] = theirs
        ours_ref[...] = ours
        for value, ref in ((theirs, theirs_ref.at[pl.ds(half, 8)]), (ours, peak_ref)):
            peak = jnp.max(jnp.abs(value), axis=0, keepdims=True)
            ref[...] = jnp.broadcast_to(peak, ref.shape)


def prepare(entries, blocks):
    smem, vmem = (pl.BlockSpec(memory_space=space) for space in (pltpu.SMEM, pltpu.VMEM))
    listed = jax.ShapeDtypeStruct((blocks.shape[0] + 2 * GROUP,), jnp.int32)
    return pl.pallas_call(
        prepare_kernel,
        in_specs=[smem, pl.BlockSpec(memory_space=pl.ANY)],
        out_specs=(vmem, smem, smem, smem, vmem),
        out_shape=(
            pltpu.VMEM(blocks.shape, blocks.dtype),
            listed,
            listed,
            jax.ShapeDtypeStruct((2,), jnp.int32),
            jax.ShapeDtypeStruct((16, BS), jnp.bfloat16),
        ),
        scratch_shapes=[pltpu.SemaphoreType.DMA(())],
        compiler_params=pltpu.CompilerParams(vmem_limit_bytes=PREPARE_LIMIT * 1024 * 1024),
        cost_estimate=pl.CostEstimate(
            flops=0, bytes_accessed=8 * blocks.size, transcendentals=0
        ),
        name="prepare",
    )(entries, blocks)


def multiply(slots, counts, parts, blocks, total, before=None):
    first, width = before is None, parts[0][0].shape[-1]
    places = [place for _, place in parts]
    smem, vmem = (pl.BlockSpec(memory_space=space) for space in (pltpu.SMEM, pltpu.VMEM))
    if first:
        out_shape = pltpu.VMEM((total + BS, width), f32)
    else:
        out_shape = tuple(
            jax.ShapeDtypeStruct((rows, width), f32) for rows in (total // 2 + 8, total // 2, 8)
        )
    return pl.pallas_call(
        lambda *refs: multiply_kernel(*refs, places=places, first=first),
        in_specs=[smem] * 2
        + [pl.BlockSpec(memory_space=pl.ANY)] * len(parts)
        + [vmem] * (1 if first else 2),
        out_specs=vmem if first else (vmem,) * 3,
        out_shape=out_shape,
        scratch_shapes=[
            pltpu.VMEM((max(sum(place) for place in places), BS, width), jnp.bfloat16),
            pltpu.SemaphoreType.DMA((len(parts),)),
        ],
        compiler_params=pltpu.CompilerParams(vmem_limit_bytes=24 * 1024 * 1024),
        cost_estimate=pl.CostEstimate(
            flops=(6 if first else 1) * 10**9, bytes_accessed=0, transcendentals=0
        ),
        name="multiply_first" if first else "multiply_rest",
    )(slots, counts, *(part for part, _ in parts), blocks, *(() if first else (before,)))


def dot(a, b, contract):
    return lax.dot_general(
        a, b, ((contract[:1], contract[1:]), ((), ())),
        precision=HIGHEST, preferred_element_type=f32,
    )


def eliminate(sym):
    size = sym.shape[0]
    tiles = size // 8
    full = (8, size)
    lane = lax.broadcasted_iota(jnp.int32, full, 1)
    sub = lax.broadcasted_iota(jnp.int32, full, 0)
    on_diagonal = [jnp.where(lane == sub + 8 * t, sym[8 * t:8 * t + 8, :], 0.0) for t in range(tiles)]
    across = sum(on_diagonal[1:], on_diagonal[0]).sum(axis=0, keepdims=True)
    across = lax.rsqrt(jnp.broadcast_to(across, full))
    state = [
        sym[8 * t:8 * t + 8, :]
        * across
        * lax.rsqrt(jnp.broadcast_to(on_diagonal[t].sum(axis=1, keepdims=True), full))
        for t in range(tiles)
    ]
    undo = 1.0 / across
    upper, inverse = [], []
    for t in range(tiles):
        k = 8 * t
        panel = (lane >= k) & (lane < k + 8)
        rows = [jnp.broadcast_to(state[t][i:i + 1, :], full) for i in range(8)]
        own = [jnp.broadcast_to(state[t][:, k + i:k + i + 1], full) for i in range(8)]
        entry = {
            (a, b): jnp.broadcast_to(own[b][a:a + 1, :], full) for a in range(8) for b in range(a, 8)
        }
        columns = {
            i: [jnp.broadcast_to(state[i][:, k + a:k + a + 1], full) for a in range(8)]
            for i in range(t + 1, tiles)
        }
        mixed = [jnp.where(panel, (lane == k + i).astype(f32), rows[i]) for i in range(8)]
        for i in range(t + 1, tiles):
            state[i] = jnp.where(panel, 0.0, state[i])

        def solve(a, x, y, inverse_of):
            p, q, r = entry[a, a], entry[a, a + 1], entry[a + 1, a + 1]
            return (r * x - q * y) * inverse_of, (p * y - q * x) * inverse_of

        recip, ratio = {}, {}
        for a in range(0, 8, 2):
            c = a + 1
            recip[a] = 1.0 / (entry[a, a] * entry[c, c] - entry[a, c] * entry[a, c])
            for b in range(a + 2, 8):
                ratio[a, b], ratio[c, b] = solve(a, entry[a, b], entry[c, b], recip[a])
            for b in range(a + 2, 8):
                for d in range(b, 8):
                    entry[b, d] = entry[b, d] - (
                        ratio[a, b] * entry[a, d] + ratio[c, b] * entry[c, d]
                    )
                mixed[b] = mixed[b] - (ratio[a, b] * mixed[a] + ratio[c, b] * mixed[c])
            if t + 1 < tiles:
                ahead = columns[t + 1]
                x, y = solve(a, ahead[a], ahead[c], recip[a])
                for b in range(a + 2, 8):
                    ahead[b] = ahead[b] - (x * entry[a, b] + y * entry[c, b])
                state[t + 1] = state[t + 1] - (x * mixed[a] + y * mixed[c])
        if t + 2 < tiles:
            back = [None] * 8
            for a in range(6, -1, -2):
                back[a], back[a + 1] = solve(a, mixed[a], mixed[a + 1], recip[a])
                for b in range(a + 2, 8):
                    back[a] = back[a] - ratio[a, b] * back[b]
                    back[a + 1] = back[a + 1] - ratio[a + 1, b] * back[b]
            for i in range(t + 2, tiles):
                for a in range(7, -1, -1):
                    state[i] = state[i] - columns[i][a] * back[a]
        for a in range(0, 8, 2):
            step = entry[a, a + 1] / entry[a, a]
            mixed[a + 1] = mixed[a + 1] - step * mixed[a]
            for b in range(7, a, -1):
                entry[a + 1, b] = entry[a + 1, b] - step * entry[a, b]
        pivot, result = entry[0, 0], mixed[0]
        for a in range(1, 8):
            pivot = jnp.where(sub == a, entry[a, a], pivot)
            result = jnp.where(sub == a, mixed[a], result)
        scale = 1.0 / jnp.sqrt(pivot)
        result = result * scale
        corner = jnp.zeros(full, f32)
        for b in range(8):
            column = entry[0, b]
            for a in range(1, b + 1):
                column = jnp.where(sub == a, entry[a, b], column)
            corner = jnp.where((lane == k + b) & (sub <= b), column * scale, corner)
        upper.append(jnp.where(lane >= k + 8, result, corner) * undo)
        inverse.append(jnp.where(lane < k + 8, result, 0.0) * across)
    return jnp.concatenate(upper, 0), jnp.concatenate(inverse, 0)


def factor_kernel(gram_ref, sketch_ref, factor_ref, basis_ref, *, scale):
    half = gram_ref.shape[1]
    top, bottom = pl.ds(0, half), pl.ds(half, half)
    upper1, inverse1 = eliminate(gram_ref[top, :])
    cross = dot(inverse1, gram_ref[bottom, :], (1, 0))
    upper2, inverse2 = eliminate(gram_ref[pl.ds(2 * half, half), :] - dot(cross, cross, (0, 0)))
    factor_ref[top, top] = upper1 * (1.0 / scale)
    factor_ref[top, bottom] = cross * (1.0 / scale)
    factor_ref[bottom, top] = jnp.zeros((half, half), f32)
    factor_ref[bottom, bottom] = upper2 * (1.0 / scale)
    first = dot(sketch_ref[:, top], inverse1, (1, 1))
    rest = sketch_ref[:, bottom] - dot(first, cross, (1, 0))
    basis_ref[:, top] = first * scale
    basis_ref[:, bottom] = dot(rest, inverse2, (1, 1)) * scale


def orthonormalize(gram, sketch, vertex_total):
    return pl.pallas_call(
        lambda *refs: factor_kernel(*refs, scale=math.sqrt(vertex_total)),
        out_shape=(
            jax.ShapeDtypeStruct((sketch.shape[1],) * 2, f32),
            jax.ShapeDtypeStruct(sketch.shape, f32),
        ),
        compiler_params=pltpu.CompilerParams(vmem_limit_bytes=32 * 1024 * 1024),
        name="orthonormalize",
    )(gram, sketch)


def spread(value, axes, count):
    copies = jnp.broadcast_to(value[None], (count,) + value.shape)
    return lax.all_to_all(copies, axes, 0, 0, tiled=True)


def sum_over_all(gram):
    half = gram.shape[0] // 2
    packed = jnp.concatenate([gram[:half, :half], gram[:half, half:], gram[half:, half:]], 0)
    pieces = packed.reshape(16, -1, half)
    part = lax.all_to_all(pieces, ("y", "x"), 0, 0, tiled=True).sum(0)
    part = part + shift(part, "core", 1)
    part = spread(part, ("z",), 8).sum(0)
    return spread(part, ("y", "x"), 16).reshape(packed.shape)


def split_shift(value, axis):
    size = SIZES[axis]
    pairs = []
    for i in range(size):
        pairs += [(2 * i, 2 * ((i + 1) % size)), (2 * i + 1, 2 * ((i - 1) % size) + 1)]
    return lax.ppermute(value, (axis, "core"), pairs)


def gather(omega, token):
    half = omega.shape[0] // 2

    def short_way(both, axis):
        count = SIZES[axis] // 2
        steps = [both]
        for _ in range(count - 1):
            steps.append(split_shift(steps[-1], axis))
        end = split_shift(steps[-1][:1], axis)
        others = shift(jnp.concatenate([step[1:] for step in steps[1:]], 0), "core", 1)
        near = [step[:1] for step in steps]
        return jnp.concatenate([near[0], others, end] + near[:0:-1], 0)

    def ring(block, axis, token=None):
        size = SIZES[axis]
        forth, back, found = block, block, {0: block}
        for step in range(1, size // 2):
            forth, back = shift(forth, axis, 1), shift(back, axis, -1)
            if step == 1 and token is not None:
                forth, token = lax.optimization_barrier((forth, token))
            found[size - step], found[step] = forth, back
        return found, forth, back

    def last(forth, back, axis):
        cut = forth.shape[0] // 2
        return shift(forth[:cut], axis, 1), shift(back[cut:], axis, -1)

    both = jnp.stack([omega, shift(omega, "core", 1)])
    block1, block2 = short_way(both[:, :half], "y"), short_way(both[:, half:], "z")
    full1, forth1, back1 = ring(block1, "z")
    block2, token = lax.optimization_barrier((block2, token))
    full2, forth2, back2 = ring(block2, "y")
    end1, end2 = last(forth1, back1, "z"), last(forth2, back2, "y")
    early = [(full1[dz], (4 * dz, 4)) for dz in (0, 7, 1, 6, 2, 5, 3)]
    early += [(full2[dy], (32 + 8 * dy, 8)) for dy in (0, 3, 1)]
    late = [(end1[0], (0, 2)), (end1[1], (2, 2)), (end2[0], (4, 4)), (end2[1], (8, 4))]
    return early, late


def sum_over_columns(theirs, ours, peak):
    received = shift(theirs, "core", 1)
    count = ours.shape[0]
    ours = ours + received[:count]
    rows = count // 4
    bound = jnp.maximum(peak[:1] + received[count:count + 1], 1e-30)
    exponent = jnp.ceil(jnp.log2(bound)) - 13.0
    sent = ours[rows:] * jnp.exp2(-exponent)
    exponents = jnp.broadcast_to(exponent, (16, exponent.shape[1]))
    result = ours[:rows]
    for k in (2, 1, 3):
        term = jnp.concatenate([sent[(k - 1) * rows:k * rows], exponents], 0)
        term = shift(term.astype(jnp.float16), "x", k).astype(f32)
        result = result + term[:rows] * jnp.exp2(term[rows:rows + 1])
    return result


def shards(blocks, block_rows, block_cols, live_counts, omega, row_scale):
    own_rows, width = omega.shape
    row_blocks = own_rows * 8 // BS
    per = own_rows // BS
    x_here, core_here = lax.axis_index("x"), lax.axis_index("core")
    rows, cols, count = block_rows[0, 0], block_cols[0, 0], live_counts[0, 0]
    x_of, core_of, rest = rows // (2 * per), (rows // per) % 2, rows % per
    rows = (
        jnp.where(core_of == core_here, 4 * per, 0) + ((x_of - x_here + 4) % 4) * per + rest
    )
    z_here, y_here = lax.axis_index("z"), lax.axis_index("y")
    far_z, far_y = (cols // 8 - z_here + 8) % 8, (cols // 2 - y_here + 4) % 4
    is_second = cols % 2
    is_late = jnp.where(is_second == 1, far_y == 2, far_z == 4)
    back = core_here == 1
    far_z = jnp.where(back & (is_second == 1), (8 - far_z) % 8, far_z)
    far_y = jnp.where(back & (is_second == 0), (4 - far_y) % 4, far_y)
    cols = jnp.where(
        is_late,
        jnp.where(is_second == 1, 4 + far_z, far_y),
        jnp.where(is_second == 1, 32 + 8 * far_y + far_z, 4 * far_z + far_y),
    )
    slot = jnp.arange(rows.shape[0], dtype=jnp.int32)
    kind = jnp.where(slot < count, is_late.astype(jnp.int32), 2)
    entries = slot + 256 * rows + 8192 * cols + KIND * kind
    held, early_list, late_list, counts, token = prepare(entries, blocks[0, 0])
    early, late = gather(omega, token)
    total = row_blocks * BS
    before = multiply(early_list, counts, early, held, total)
    theirs, ours, peak = multiply(late_list, counts, late, held, total, before)
    sketch = sum_over_columns(theirs, ours, peak)
    sketch = sketch * row_scale[:, None]
    gram = sum_over_all(dot(sketch, sketch, (0, 0)))
    factor, basis = orthonormalize(gram, sketch, own_rows * 256)
    return (basis, factor)


def solution(mesh):
    fine = Mesh(mesh.devices.reshape(8, 4, 4, 2), ("z", "y", "x", "core"))
    row, col = ("z", "y"), ("x", "core")
    placed = (
        P(row, col, None, None, None),
        P(row, col, None),
        P(row, col, None),
        P(row, col),
        P(col + row, None),
        P(row + col),
    )
    return jax.shard_map(
        shards,
        mesh=fine,
        in_specs=placed,
        out_specs=(P(row + col, None), P()),
        check_vma=False,
    )
```

```python
import math

import jax
import jax.numpy as jnp
from jax import lax
from jax.experimental import pallas as pl
from jax.experimental.pallas import tpu as pltpu
from jax.sharding import Mesh
from jax.sharding import PartitionSpec as P

f32 = jnp.float32
HIGHEST = lax.Precision.HIGHEST
BS = 128
GROUP = 16
KIND = 1 << 20
PREPARE_LIMIT = 46
SIZES = {"z": 8, "y": 4, "x": 4, "core": 2}


def shift(value, axis, step):
    size = SIZES[axis]
    return lax.ppermute(value, axis, [(i, (i + step) % size) for i in range(size)])


def add_groups(groups, end, list_ref, blocks_ref, omega_ref, out_ref):
    spare = (out_ref.shape[0] // BS - 1) * 256

    def group(step, carry):
        for index in range(GROUP):
            place = step * GROUP + index
            entry = jnp.where(place < end, list_ref[place], spare)
            row = pl.multiple_of(((entry >> 8) & 31) * BS, BS)
            out_ref[pl.ds(row, BS), :] += jnp.dot(
                blocks_ref[entry & 255], omega_ref[entry >> 13], preferred_element_type=f32
            )
        return carry

    lax.fori_loop(*groups, group, 0)


def copies_of(part_refs, places, omega_ref, sems):
    return [
        pltpu.make_async_copy(part_refs[index], omega_ref.at[pl.ds(*place)], sems.at[index])
        for index, place in enumerate(places)
    ]


def prepare_kernel(entries_ref, source_ref, blocks_ref, early_ref, late_ref, counts_ref, token_ref, sem):
    load = pltpu.make_async_copy(source_ref, blocks_ref, sem)
    load.start()
    token_ref[...] = jnp.zeros_like(token_ref)

    def sort(slot, counts):
        early, late = counts
        entry = entries_ref[slot]
        kind = entry >> 20
        early_ref[early] = entry
        late_ref[late] = entry & (KIND - 1)
        return early + ((kind + 3) >> 2 ^ 1), late + (kind & 1)

    start = jnp.int32(0), jnp.int32(0)
    counts_ref[0], counts_ref[1] = lax.fori_loop(0, blocks_ref.shape[0], sort, start, unroll=8)
    load.wait()


def multiply_kernel(list_ref, counts_ref, *refs, places, first):
    part_refs = refs[:len(places)]
    blocks_ref, omega_ref, sems = refs[len(places)], *refs[-2:]
    copies = copies_of(part_refs, places, omega_ref, sems)
    for copy in copies:
        copy.start()
    if first:
        out_ref = refs[len(places) + 1]
        out_ref[...] = jnp.zeros_like(out_ref)
    else:
        out_ref, theirs_ref, ours_ref, peak_ref = refs[len(places) + 1:-2]
    for copy in copies:
        copy.wait()
    count = counts_ref[0 if first else 1]
    groups = 0, (count + GROUP - 1) // GROUP
    add_groups(groups, count, list_ref, blocks_ref, omega_ref, out_ref)
    if not first:
        half = ours_ref.shape[0]
        theirs, ours = out_ref[pl.ds(0, half), :], out_ref[pl.ds(half, half), :]
        theirs_ref[pl.ds(0, half), :] = theirs
        ours_ref[...] = ours
        for value, ref in ((theirs, theirs_ref.at[pl.ds(half, 8)]), (ours, peak_ref)):
            peak = jnp.max(jnp.abs(value), axis=0, keepdims=True)
            ref[...] = jnp.broadcast_to(peak, ref.shape)


def prepare(entries, blocks):
    smem, vmem = (pl.BlockSpec(memory_space=space) for space in (pltpu.SMEM, pltpu.VMEM))
    listed = jax.ShapeDtypeStruct((blocks.shape[0] + 2 * GROUP,), jnp.int32)
    return pl.pallas_call(
        prepare_kernel,
        in_specs=[smem, pl.BlockSpec(memory_space=pl.ANY)],
        out_specs=(vmem, smem, smem, smem, vmem),
        out_shape=(
            pltpu.VMEM(blocks.shape, blocks.dtype),
            listed,
            listed,
            jax.ShapeDtypeStruct((2,), jnp.int32),
            jax.ShapeDtypeStruct((16, BS), jnp.bfloat16),
        ),
        scratch_shapes=[pltpu.SemaphoreType.DMA(())],
        compiler_params=pltpu.CompilerParams(vmem_limit_bytes=PREPARE_LIMIT * 1024 * 1024),
        cost_estimate=pl.CostEstimate(
            flops=0, bytes_accessed=8 * blocks.size, transcendentals=0
        ),
        name="prepare",
    )(entries, blocks)


def multiply(slots, counts, parts, blocks, total, before=None):
    first, width = before is None, parts[0][0].shape[-1]
    places = [place for _, place in parts]
    smem, vmem = (pl.BlockSpec(memory_space=space) for space in (pltpu.SMEM, pltpu.VMEM))
    if first:
        out_shape = pltpu.VMEM((total + BS, width), f32)
    else:
        out_shape = tuple(
            jax.ShapeDtypeStruct((rows, width), f32) for rows in (total // 2 + 8, total // 2, 8)
        )
    return pl.pallas_call(
        lambda *refs: multiply_kernel(*refs, places=places, first=first),
        in_specs=[smem] * 2
        + [pl.BlockSpec(memory_space=pl.ANY)] * len(parts)
        + [vmem] * (1 if first else 2),
        out_specs=vmem if first else (vmem,) * 3,
        out_shape=out_shape,
        scratch_shapes=[
            pltpu.VMEM((max(sum(place) for place in places), BS, width), jnp.bfloat16),
            pltpu.SemaphoreType.DMA((len(parts),)),
        ],
        compiler_params=pltpu.CompilerParams(vmem_limit_bytes=24 * 1024 * 1024),
        cost_estimate=pl.CostEstimate(
            flops=(6 if first else 1) * 10**9, bytes_accessed=0, transcendentals=0
        ),
        name="multiply_first" if first else "multiply_rest",
    )(slots, counts, *(part for part, _ in parts), blocks, *(() if first else (before,)))


def dot(a, b, contract):
    return lax.dot_general(
        a, b, ((contract[:1], contract[1:]), ((), ())),
        precision=HIGHEST, preferred_element_type=f32,
    )


def eliminate(sym):
    size = sym.shape[0]
    tiles = size // 8
    full = (8, size)
    lane = lax.broadcasted_iota(jnp.int32, full, 1)
    sub = lax.broadcasted_iota(jnp.int32, full, 0)
    on_diagonal = [jnp.where(lane == sub + 8 * t, sym[8 * t:8 * t + 8, :], 0.0) for t in range(tiles)]
    across = sum(on_diagonal[1:], on_diagonal[0]).sum(axis=0, keepdims=True)
    across = lax.rsqrt(jnp.broadcast_to(across, full))
    state = [
        sym[8 * t:8 * t + 8, :]
        * across
        * lax.rsqrt(jnp.broadcast_to(on_diagonal[t].sum(axis=1, keepdims=True), full))
        for t in range(tiles)
    ]
    undo = 1.0 / across
    upper, inverse = [], []
    for t in range(tiles):
        k = 8 * t
        panel = (lane >= k) & (lane < k + 8)
        rows = [jnp.broadcast_to(state[t][i:i + 1, :], full) for i in range(8)]
        own = [jnp.broadcast_to(state[t][:, k + i:k + i + 1], full) for i in range(8)]
        entry = {
            (a, b): jnp.broadcast_to(own[b][a:a + 1, :], full) for a in range(8) for b in range(a, 8)
        }
        columns = {
            i: [jnp.broadcast_to(state[i][:, k + a:k + a + 1], full) for a in range(8)]
            for i in range(t + 1, tiles)
        }
        mixed = [jnp.where(panel, (lane == k + i).astype(f32), rows[i]) for i in range(8)]
        for i in range(t + 1, tiles):
            state[i] = jnp.where(panel, 0.0, state[i])

        def solve(a, x, y, inverse_of):
            p, q, r = entry[a, a], entry[a, a + 1], entry[a + 1, a + 1]
            return (r * x - q * y) * inverse_of, (p * y - q * x) * inverse_of

        recip, ratio = {}, {}
        for a in range(0, 8, 2):
            c = a + 1
            recip[a] = 1.0 / (entry[a, a] * entry[c, c] - entry[a, c] * entry[a, c])
            for b in range(a + 2, 8):
                ratio[a, b], ratio[c, b] = solve(a, entry[a, b], entry[c, b], recip[a])
            for b in range(a + 2, 8):
                for d in range(b, 8):
                    entry[b, d] = entry[b, d] - (
                        ratio[a, b] * entry[a, d] + ratio[c, b] * entry[c, d]
                    )
                mixed[b] = mixed[b] - (ratio[a, b] * mixed[a] + ratio[c, b] * mixed[c])
            if t + 1 < tiles:
                ahead = columns[t + 1]
                x, y = solve(a, ahead[a], ahead[c], recip[a])
                for b in range(a + 2, 8):
                    ahead[b] = ahead[b] - (x * entry[a, b] + y * entry[c, b])
                state[t + 1] = state[t + 1] - (x * mixed[a] + y * mixed[c])
        if t + 2 < tiles:
            back = [None] * 8
            for a in range(6, -1, -2):
                back[a], back[a + 1] = solve(a, mixed[a], mixed[a + 1], recip[a])
                for b in range(a + 2, 8):
                    back[a] = back[a] - ratio[a, b] * back[b]
                    back[a + 1] = back[a + 1] - ratio[a + 1, b] * back[b]
            for i in range(t + 2, tiles):
                for a in range(7, -1, -1):
                    state[i] = state[i] - columns[i][a] * back[a]
        for a in range(0, 8, 2):
            step = entry[a, a + 1] / entry[a, a]
            mixed[a + 1] = mixed[a + 1] - step * mixed[a]
            for b in range(7, a, -1):
                entry[a + 1, b] = entry[a + 1, b] - step * entry[a, b]
        pivot, result = entry[0, 0], mixed[0]
        for a in range(1, 8):
            pivot = jnp.where(sub == a, entry[a, a], pivot)
            result = jnp.where(sub == a, mixed[a], result)
        scale = 1.0 / jnp.sqrt(pivot)
        result = result * scale
        corner = jnp.zeros(full, f32)
        for b in range(8):
            column = entry[0, b]
            for a in range(1, b + 1):
                column = jnp.where(sub == a, entry[a, b], column)
            corner = jnp.where((lane == k + b) & (sub <= b), column * scale, corner)
        upper.append(jnp.where(lane >= k + 8, result, corner) * undo)
        inverse.append(jnp.where(lane < k + 8, result, 0.0) * across)
    return jnp.concatenate(upper, 0), jnp.concatenate(inverse, 0)


def factor_kernel(gram_ref, sketch_ref, factor_ref, basis_ref, *, scale):
    half = gram_ref.shape[1]
    top, bottom = pl.ds(0, half), pl.ds(half, half)
    upper1, inverse1 = eliminate(gram_ref[top, :])
    cross = dot(inverse1, gram_ref[bottom, :], (1, 0))
    upper2, inverse2 = eliminate(gram_ref[pl.ds(2 * half, half), :] - dot(cross, cross, (0, 0)))
    factor_ref[top, top] = upper1 * (1.0 / scale)
    factor_ref[top, bottom] = cross * (1.0 / scale)
    factor_ref[bottom, top] = jnp.zeros((half, half), f32)
    factor_ref[bottom, bottom] = upper2 * (1.0 / scale)
    first = dot(sketch_ref[:, top], inverse1, (1, 1))
    rest = sketch_ref[:, bottom] - dot(first, cross, (1, 0))
    basis_ref[:, top] = first * scale
    basis_ref[:, bottom] = dot(rest, inverse2, (1, 1)) * scale


def orthonormalize(gram, sketch, vertex_total):
    return pl.pallas_call(
        lambda *refs: factor_kernel(*refs, scale=math.sqrt(vertex_total)),
        out_shape=(
            jax.ShapeDtypeStruct((sketch.shape[1],) * 2, f32),
            jax.ShapeDtypeStruct(sketch.shape, f32),
        ),
        compiler_params=pltpu.CompilerParams(vmem_limit_bytes=32 * 1024 * 1024),
        name="orthonormalize",
    )(gram, sketch)


def spread(value, axes, count):
    copies = jnp.broadcast_to(value[None], (count,) + value.shape)
    return lax.all_to_all(copies, axes, 0, 0, tiled=True)


def sum_over_all(gram):
    half = gram.shape[0] // 2
    packed = jnp.concatenate([gram[:half, :half], gram[:half, half:], gram[half:, half:]], 0)
    pieces = packed.reshape(16, -1, half)
    part = lax.all_to_all(pieces, ("y", "x"), 0, 0, tiled=True).sum(0)
    part = part + shift(part, "core", 1)
    part = spread(part, ("z",), 8).sum(0)
    return spread(part, ("y", "x"), 16).reshape(packed.shape)


def split_shift(value, axis):
    size = SIZES[axis]
    pairs = []
    for i in range(size):
        pairs += [(2 * i, 2 * ((i + 1) % size)), (2 * i + 1, 2 * ((i - 1) % size) + 1)]
    return lax.ppermute(value, (axis, "core"), pairs)


def gather(omega, token):
    half = omega.shape[0] // 2

    def short_way(both, axis):
        count = SIZES[axis] // 2
        steps = [both]
        for _ in range(count - 1):
            steps.append(split_shift(steps[-1], axis))
        end = split_shift(steps[-1][:1], axis)
        others = shift(jnp.concatenate([step[1:] for step in steps[1:]], 0), "core", 1)
        near = [step[:1] for step in steps]
        return jnp.concatenate([near[0], others, end] + near[:0:-1], 0)

    def ring(block, axis, token=None):
        size = SIZES[axis]
        forth, back, found = block, block, {0: block}
        for step in range(1, size // 2):
            forth, back = shift(forth, axis, 1), shift(back, axis, -1)
            if step == 1 and token is not None:
                forth, token = lax.optimization_barrier((forth, token))
            found[size - step], found[step] = forth, back
        return found, forth, back

    def last(forth, back, axis):
        cut = forth.shape[0] // 2
        return shift(forth[:cut], axis, 1), shift(back[cut:], axis, -1)

    other = shift(omega, "core", 1)
    block2 = short_way(jnp.stack([omega[half:], other[half:]]), "z")
    block1 = short_way(jnp.stack([omega[:half], other[:half]]), "y")
    full1, forth1, back1 = ring(block1, "z")
    block2, token = lax.optimization_barrier((block2, token))
    full2, forth2, back2 = ring(block2, "y")
    end1, end2 = last(forth1, back1, "z"), last(forth2, back2, "y")
    early = [(full1[dz], (4 * dz, 4)) for dz in (0, 7, 1, 6, 2, 5, 3)]
    early += [(full2[dy], (32 + 8 * dy, 8)) for dy in (0, 3, 1)]
    late = [(end1[0], (0, 2)), (end1[1], (2, 2)), (end2[0], (4, 4)), (end2[1], (8, 4))]
    return early, late


def sum_over_columns(theirs, ours, peak):
    received = shift(theirs, "core", 1)
    count = ours.shape[0]
    ours = ours + received[:count]
    rows = count // 4
    bound = jnp.maximum(peak[:1] + received[count:count + 1], 1e-30)
    exponent = jnp.ceil(jnp.log2(bound)) - 13.0
    sent = ours[rows:] * jnp.exp2(-exponent)
    exponents = jnp.broadcast_to(exponent, (16, exponent.shape[1]))
    result = ours[:rows]
    for k in (2, 1, 3):
        term = jnp.concatenate([sent[(k - 1) * rows:k * rows], exponents], 0)
        term = shift(term.astype(jnp.float16), "x", k).astype(f32)
        result = result + term[:rows] * jnp.exp2(term[rows:rows + 1])
    return result


def shards(blocks, block_rows, block_cols, live_counts, omega, row_scale):
    own_rows, width = omega.shape
    row_blocks = own_rows * 8 // BS
    per = own_rows // BS
    x_here, core_here = lax.axis_index("x"), lax.axis_index("core")
    rows, cols, count = block_rows[0, 0], block_cols[0, 0], live_counts[0, 0]
    x_of, core_of, rest = rows // (2 * per), (rows // per) % 2, rows % per
    rows = (
        jnp.where(core_of == core_here, 4 * per, 0) + ((x_of - x_here + 4) % 4) * per + rest
    )
    z_here, y_here = lax.axis_index("z"), lax.axis_index("y")
    far_z, far_y = (cols // 8 - z_here + 8) % 8, (cols // 2 - y_here + 4) % 4
    is_second = cols % 2
    is_late = jnp.where(is_second == 1, far_y == 2, far_z == 4)
    back = core_here == 1
    far_z = jnp.where(back & (is_second == 1), (8 - far_z) % 8, far_z)
    far_y = jnp.where(back & (is_second == 0), (4 - far_y) % 4, far_y)
    cols = jnp.where(
        is_late,
        jnp.where(is_second == 1, 4 + far_z, far_y),
        jnp.where(is_second == 1, 32 + 8 * far_y + far_z, 4 * far_z + far_y),
    )
    slot = jnp.arange(rows.shape[0], dtype=jnp.int32)
    kind = jnp.where(slot < count, is_late.astype(jnp.int32), 2)
    entries = slot + 256 * rows + 8192 * cols + KIND * kind
    held, early_list, late_list, counts, token = prepare(entries, blocks[0, 0])
    early, late = gather(omega, token)
    total = row_blocks * BS
    before = multiply(early_list, counts, early, held, total)
    theirs, ours, peak = multiply(late_list, counts, late, held, total, before)
    sketch = sum_over_columns(theirs, ours, peak)
    sketch = sketch * row_scale[:, None]
    gram = sum_over_all(dot(sketch, sketch, (0, 0)))
    factor, basis = orthonormalize(gram, sketch, own_rows * 256)
    return (basis, factor)


def solution(mesh):
    fine = Mesh(mesh.devices.reshape(8, 4, 4, 2), ("z", "y", "x", "core"))
    row, col = ("z", "y"), ("x", "core")
    placed = (
        P(row, col, None, None, None),
        P(row, col, None),
        P(row, col, None),
        P(row, col),
        P(col + row, None),
        P(row + col),
    )
    return jax.shard_map(
        shards,
        mesh=fine,
        in_specs=placed,
        out_specs=(P(row + col, None), P()),
        check_vma=False,
    )
```
